256 devices in a mesh: dp: 32 (over z, x), tensor: 8 (over y, core).
Axes of the slice: x: 4, y: 4, z: 8, core: 2. Of those that a mesh axis runs over, the one named last changes fastest.
Arguments:
- tokens: bfloat16 [65536, 8192], P('dp', 'tensor'), may hold values from -6 to 6
- value_projection_weight: bfloat16 [8192, 1024], P('tensor'), may hold values from -0.0625 to 0.0625
- adapter_down_factors: bfloat16 [1024, 8192, 64], P('dp', 'tensor'), may hold values from -0.0625 to 0.0625
- adapter_up_factors: bfloat16 [1024, 64, 1024], P('dp', None, 'tensor'), may hold values from -0.75 to 0.75
- block_adapter_table: int32 [32, 16], P('dp'), may hold values from 0 to 1023, as said below
Outputs:
- values_out: bfloat16 [65536, 1024], P('dp', 'tensor')
The draws below stay inside these ranges and needn't reach their ends.
Inputs may be any that keep to these rules, and one draw needn't show every extreme that they name: `block_adapter_table`: adapter a is owned by index a // 32 of dp. In each microbatch no dp index owns the adapters of more than 1 block, and each dp index that owns any of them owns exactly 1.
All inputs are finite; a program needn't handle non-finite values.
Results may differ from the reference program's by a relative error of at most 0.0039.
Values may be sent and summed in bfloat16 or wider, within the bound.
No kernel may reach another device: no remote copies, remote signals or barrier semaphores. Data moves between devices by JAX's collectives and lax.ppermute only.
A program may use at most 128 MiB of HBM per device.

```python
import jax
import jax.numpy as jnp
from jax import lax

HIDDEN_WIDTH = 8192
VALUE_WIDTH = 1024
LOW_RANK_SIZE = 64
ADP_DEV = 32
BLOCK = 128
BLOCKS = 16
CAP = 1
MICROBATCH_COUNT = 32
ADAPTER_TOTAL = 1024
TOKENS = 65536


def shuffle_row(row_key):
    return jax.random.permutation(row_key, BLOCKS)


def draw_block_adapter_table(key, part):
    key = jax.random.fold_in(key, 7)
    key_pop, key_jit, key_perm, key_local = jax.random.split(key, 4)
    popularity = jax.random.randint(key_pop, (MICROBATCH_COUNT,), 0, 4)
    jitter_vals = jax.random.randint(key_jit, (MICROBATCH_COUNT, MICROBATCH_COUNT), 0, 8)
    score_values = (popularity[None, :] * 3 + jitter_vals) * MICROBATCH_COUNT + jnp.arange(MICROBATCH_COUNT, dtype=jnp.int32)[None, :]
    extra_term = jnp.zeros((MICROBATCH_COUNT, MICROBATCH_COUNT), jnp.int32)
    extra_term = extra_term.at[0, MICROBATCH_COUNT - 1].add(32 * MICROBATCH_COUNT)
    extra_term = extra_term.at[MICROBATCH_COUNT - 1, 0].add(32 * MICROBATCH_COUNT)
    score_values = score_values + extra_term
    chosen = lax.top_k(score_values, BLOCKS // CAP)[1]
    owners = jnp.repeat(chosen, CAP, axis=1)
    shuffle = jax.vmap(shuffle_row)(jax.random.split(key_perm, MICROBATCH_COUNT))
    owners = jnp.take_along_axis(owners, shuffle, axis=1)
    local_ids = jax.random.randint(key_local, (MICROBATCH_COUNT, BLOCKS), 0, ADP_DEV)
    row_index = jnp.arange(MICROBATCH_COUNT, dtype=jnp.int32)[:, None]
    local_ids = jnp.where((row_index == 0) & (owners == MICROBATCH_COUNT - 1), ADP_DEV - 1, local_ids)
    local_ids = jnp.where((row_index == MICROBATCH_COUNT - 1) & (owners == 0), 0, local_ids)
    return (owners * ADP_DEV + local_ids).astype(jnp.int32)


def block_levels(own_key, shape, cuts, least, top_value):
    gain = 1.0
    for dim, shards_of in cuts:
        steps = jax.random.uniform(jax.random.fold_in(jax.random.fold_in(own_key, 6), dim), (shards_of,), jnp.float32, least / len(cuts), top_value / len(cuts))
        gain = gain * jnp.repeat(jnp.exp(steps), shape[dim] // shards_of).reshape((-1,) + (1,) * (len(shape) - 1 - dim))
    return gain


def centred(own_key, shape, scale, most, pieces=(), kind=jnp.bfloat16):
    gain = block_levels(own_key, shape, pieces, -0.22, 0.18) if pieces else 1.0
    entries = jax.random.normal(own_key, shape, jnp.float32) * scale * gain
    return jnp.minimum(jnp.maximum(entries, -most), most).astype(kind)


def setup_inputs(seed: int = 0) -> dict:
    splits = jax.random.split(jax.random.key(seed), 6)
    tokens = centred(splits[0], (TOKENS, HIDDEN_WIDTH), 1.0, 6.0, ((0, 32), (1, 8)))
    value_projection_weight = centred(splits[1], (HIDDEN_WIDTH, VALUE_WIDTH), HIDDEN_WIDTH ** -0.5, 0.0625, ((0, 8),))
    adapter_down_factors = centred(splits[2], (ADAPTER_TOTAL, HIDDEN_WIDTH, LOW_RANK_SIZE), HIDDEN_WIDTH ** -0.5, 0.0625, ((0, 32), (1, 8)))
    adapter_up_factors = centred(splits[3], (ADAPTER_TOTAL, LOW_RANK_SIZE, VALUE_WIDTH), LOW_RANK_SIZE ** -0.5, 0.75, ((0, 32), (2, 8)))
    block_adapter_table = draw_block_adapter_table(jax.random.fold_in(splits[5], 71), 0)
    return dict(tokens=tokens, value_projection_weight=value_projection_weight, adapter_down_factors=adapter_down_factors, adapter_up_factors=adapter_up_factors, block_adapter_table=block_adapter_table)


def reference(tokens, value_projection_weight, adapter_down_factors, adapter_up_factors, block_adapter_table):
    base = jnp.dot(tokens, value_projection_weight, preferred_element_type=jnp.float32)
    adapter_ids = block_adapter_table.reshape(-1).astype(jnp.int32)
    token_blocks = tokens.reshape(-1, BLOCK, HIDDEN_WIDTH)

    def one_block(pair):
        input_rows, adapter_choice_id = pair
        down_factor_rows = jnp.dot(input_rows, adapter_down_factors[adapter_choice_id], preferred_element_type=jnp.float32)
        low_rank_output = down_factor_rows.astype(jnp.bfloat16)
        return jnp.dot(low_rank_output, adapter_up_factors[adapter_choice_id], preferred_element_type=jnp.float32)

    delta = lax.map(one_block, (token_blocks, adapter_ids)).reshape(-1, VALUE_WIDTH)
    return (base + delta).astype(jnp.bfloat16)
```

```python
import jax
import jax.numpy as jnp
from jax import lax
from jax.experimental import pallas as pl
from jax.experimental.pallas import tpu as pltpu
from jax.sharding import PartitionSpec as P

BLOCK = 128


def pick_kernel(ids_ref, down_ref, up_ref, out_ref, buf, insem, outsem):
    slots, rank, width = out_ref.shape
    feat = down_ref.shape[2]
    loads = []
    stores = []
    for s in range(slots):
        i = ids_ref[s, 0]
        loads.append(
            (
                pltpu.make_async_copy(
                    down_ref.at[i], buf.at[s, :, pl.ds(0, feat)], insem.at[0, s]
                ),
                pltpu.make_async_copy(
                    up_ref.at[i], buf.at[s, :, pl.ds(feat, width - feat)], insem.at[1, s]
                ),
            )
        )
        stores.append(pltpu.make_async_copy(buf.at[s], out_ref.at[s], outsem.at[s]))
    for pair in loads:
        for c in pair:
            c.start()
    for pair, store in zip(loads, stores):
        for c in pair:
            c.wait()
        store.start()
    for store in stores:
        store.wait()


def pick(ids, down_t, up):
    slots = ids.shape[0]
    _, rank, feat = down_t.shape
    width = feat + up.shape[2]
    return pl.pallas_call(
        pick_kernel,
        out_shape=jax.ShapeDtypeStruct((slots, rank, width), down_t.dtype),
        in_specs=[
            pl.BlockSpec(memory_space=pltpu.SMEM),
            pl.BlockSpec(memory_space=pltpu.HBM),
            pl.BlockSpec(memory_space=pltpu.HBM),
        ],
        out_specs=pl.BlockSpec(memory_space=pltpu.HBM),
        scratch_shapes=[
            pltpu.VMEM((slots, rank, width), down_t.dtype),
            pltpu.SemaphoreType.DMA((2, slots)),
            pltpu.SemaphoreType.DMA((slots,)),
        ],
        compiler_params=pltpu.CompilerParams(vmem_limit_bytes=62 * 1024 * 1024),
    )(ids, down_t, up)


def down_kernel(owner_ref, tok_ref, recv_ref, part_ref, up_ref, tok, fac, tsem, fsem):
    blocks, rows, feat = tok.shape
    tcopies = []
    fcopies = []
    for b in range(blocks):
        fcopies.append(
            pltpu.make_async_copy(recv_ref.at[owner_ref[b]], fac.at[b], fsem.at[b])
        )
        tcopies.append(pltpu.make_async_copy(tok_ref.at[b], tok.at[b], tsem.at[b]))
    for b in range(blocks):
        fcopies[b].start()
        tcopies[b].start()
    for b in range(blocks):
        fcopies[b].wait()
        tcopies[b].wait()
        part_ref[b] = lax.dot_general(
            fac[b, :, :feat],
            tok[b],
            (((1,), (1,)), ((), ())),
            preferred_element_type=jnp.float32,
        ).astype(jnp.bfloat16)
        up_ref[b] = fac[b, :, feat:]


def down_products(owner, token_blocks, recv):
    blocks, rows, feat = token_blocks.shape
    _, rank, width = recv.shape
    vmem = pl.BlockSpec(memory_space=pltpu.VMEM)
    hbm = pl.BlockSpec(memory_space=pltpu.HBM)
    return pl.pallas_call(
        down_kernel,
        out_shape=(
            jax.ShapeDtypeStruct((blocks, rank, rows), jnp.bfloat16),
            jax.ShapeDtypeStruct((blocks, rank, width - feat), jnp.bfloat16),
        ),
        in_specs=[pl.BlockSpec(memory_space=pltpu.SMEM), hbm, hbm],
        out_specs=(vmem, vmem),
        scratch_shapes=[
            pltpu.VMEM((blocks, rows, feat), jnp.bfloat16),
            pltpu.VMEM((blocks, rank, width), jnp.bfloat16),
            pltpu.SemaphoreType.DMA((blocks,)),
            pltpu.SemaphoreType.DMA((blocks,)),
        ],
        compiler_params=pltpu.CompilerParams(vmem_limit_bytes=62 * 1024 * 1024),
    )(owner, token_blocks, recv)


def final_kernel(parts_ref, up_ref, base_ref, out_ref, parts, base, psem, bsem):
    blocks, shares, rank, rows = parts.shape
    pcopies = []
    bcopies = []
    for b in range(blocks):
        span = pl.ds(b * rows, rows)
        pcopies.append(pltpu.make_async_copy(parts_ref.at[:, b], parts.at[b], psem.at[b]))
        bcopies.append(
            pltpu.make_async_copy(base_ref.at[span, :], base.at[span, :], bsem.at[b])
        )
    for b in range(blocks):
        pcopies[b].start()
        bcopies[b].start()
    for b in range(blocks):
        span = pl.ds(b * rows, rows)
        pcopies[b].wait()
        total = parts[b, 0].astype(jnp.float32)
        for s in range(1, shares):
            total += parts[b, s].astype(jnp.float32)
        delta = lax.dot_general(
            total.astype(jnp.bfloat16),
            up_ref[b],
            (((0,), (0,)), ((), ())),
            preferred_element_type=jnp.float32,
        )
        bcopies[b].wait()
        out_ref[span, :] = (base[span, :] + delta).astype(jnp.bfloat16)


def finish(parts, up_blocks, base):
    shares, blocks, rank, rows = parts.shape
    vmem = pl.BlockSpec(memory_space=pltpu.VMEM)
    hbm = pl.BlockSpec(memory_space=pltpu.HBM)
    return pl.pallas_call(
        final_kernel,
        out_shape=jax.ShapeDtypeStruct(base.shape, jnp.bfloat16),
        in_specs=[hbm, vmem, hbm],
        out_specs=vmem,
        scratch_shapes=[
            pltpu.VMEM((blocks, shares, rank, rows), parts.dtype),
            pltpu.VMEM(base.shape, base.dtype),
            pltpu.SemaphoreType.DMA((blocks,)),
            pltpu.SemaphoreType.DMA((blocks,)),
        ],
        compiler_params=pltpu.CompilerParams(vmem_limit_bytes=62 * 1024 * 1024),
    )(parts, up_blocks, base)


def local(
    tokens, value_projection_weight, adapter_down_factors, adapter_up_factors, block_adapter_table
):
    groups = lax.axis_size("dp")
    rows_dev, feat_dev = tokens.shape
    blocks = rows_dev // BLOCK
    adapter_per_device = adapter_down_factors.shape[0]
    ids = block_adapter_table[0]
    owner = ids // adapter_per_device
    hit = owner[None, :] == jnp.arange(groups, dtype=jnp.int32)[:, None]
    asked = jnp.sum(jnp.where(hit, (ids - owner * adapter_per_device)[None, :], 0), axis=1)
    wanted = lax.all_to_all(asked[:, None], "dp", split_axis=0, concat_axis=0, tiled=True)
    outgoing = pick(wanted, jnp.swapaxes(adapter_down_factors, 1, 2), adapter_up_factors)
    base_part = jnp.dot(tokens, value_projection_weight, preferred_element_type=jnp.float32)
    outgoing, base_part = lax.optimization_barrier((outgoing, base_part))
    received = lax.all_to_all(outgoing, "dp", split_axis=0, concat_axis=0, tiled=True)
    base = lax.psum_scatter(base_part, "tensor", scatter_dimension=1, tiled=True)
    received, base = lax.optimization_barrier((received, base))
    part, up_blocks = down_products(owner, tokens.reshape(blocks, BLOCK, feat_dev), received)
    parts = lax.all_gather(part, "tensor", axis=0)
    return finish(parts, up_blocks, base)


def solution(mesh):
    placed = (
        P("dp", "tensor"),
        P("tensor", None),
        P("dp", "tensor", None),
        P("dp", None, "tensor"),
        P("dp", None),
    )
    return jax.shard_map(
        local, mesh=mesh, in_specs=placed, out_specs=P("dp", "tensor"), check_vma=False
    )
```

```python
import jax
import jax.numpy as jnp
from jax import lax
from jax.experimental import pallas as pl
from jax.experimental.pallas import tpu as pltpu
from jax.sharding import PartitionSpec as P

BLOCK = 128


VMEM_LIMIT = pltpu.CompilerParams(vmem_limit_bytes=62 * 1024 * 1024)
SMEM_SPEC = pl.BlockSpec(memory_space=pltpu.SMEM)
HBM_SPEC = pl.BlockSpec(memory_space=pltpu.HBM)
VMEM_SPEC = pl.BlockSpec(memory_space=pltpu.VMEM)


def pick_kernel(ids_ref, src_ref, out_ref, buf, insem, outsem):
    slots = buf.shape[0]
    groups = insem.shape[0]
    size = slots // groups
    for s in range(slots):
        pltpu.make_async_copy(src_ref.at[ids_ref[s, 0]], buf.at[s], insem.at[s // size]).start()
    stores = []
    for g in range(groups):
        span = pl.ds(g * size, size)
        pltpu.make_async_copy(src_ref.at[span], buf.at[span], insem.at[g]).wait()
        stores.append(pltpu.make_async_copy(buf.at[span], out_ref.at[span], outsem.at[g]))
        stores[g].start()
    for store in stores:
        store.wait()


def pick(ids, src):
    groups = 4
    shape = (ids.shape[0],) + src.shape[1:]
    return pl.pallas_call(
        pick_kernel,
        out_shape=jax.ShapeDtypeStruct(shape, src.dtype),
        in_specs=[SMEM_SPEC, HBM_SPEC],
        out_specs=HBM_SPEC,
        scratch_shapes=[
            pltpu.VMEM(shape, src.dtype),
            pltpu.SemaphoreType.DMA((groups,)),
            pltpu.SemaphoreType.DMA((groups,)),
        ],
        compiler_params=VMEM_LIMIT,
    )(ids, src)


def down_kernel(owner_ref, tok_ref, recv_ref, part_ref, tok, fac, tsem, fsem):
    blocks = tok.shape[0]
    groups = tsem.shape[0]
    size = blocks // groups
    for g in range(groups):
        span = pl.ds(g * size, size)
        pltpu.make_async_copy(tok_ref.at[span], tok.at[span], tsem.at[g]).start()
        for b in range(g * size, (g + 1) * size):
            pltpu.make_async_copy(recv_ref.at[owner_ref[b]], fac.at[b], fsem.at[g]).start()
    for g in range(groups):
        span = pl.ds(g * size, size)
        pltpu.make_async_copy(recv_ref.at[span], fac.at[span], fsem.at[g]).wait()
        pltpu.make_async_copy(tok_ref.at[span], tok.at[span], tsem.at[g]).wait()
        for b in range(g * size, (g + 1) * size):
            part_ref[b] = lax.dot_general(
                fac[b],
                tok[b],
                (((1,), (1,)), ((), ())),
                preferred_element_type=jnp.float32,
            ).astype(jnp.bfloat16)


def down_products(owner, token_blocks, recv):
    groups = 4
    blocks, rows, feat = token_blocks.shape
    rank = recv.shape[1]
    return pl.pallas_call(
        down_kernel,
        out_shape=jax.ShapeDtypeStruct((blocks, rank, rows), jnp.bfloat16),
        in_specs=[SMEM_SPEC, HBM_SPEC, HBM_SPEC],
        out_specs=VMEM_SPEC,
        scratch_shapes=[
            pltpu.VMEM((blocks, rows, feat), jnp.bfloat16),
            pltpu.VMEM((blocks, rank, feat), jnp.bfloat16),
            pltpu.SemaphoreType.DMA((groups,)),
            pltpu.SemaphoreType.DMA((groups,)),
        ],
        compiler_params=VMEM_LIMIT,
    )(owner, token_blocks, recv)


def final_kernel(owner_ref, parts_ref, up_ref, base_ref, out_ref):
    shares, blocks, rank, rows = parts_ref.shape
    first = pl.program_id(0) * blocks
    for b in range(blocks):
        total = parts_ref[0, b].astype(jnp.float32)
        for s in range(1, shares):
            total += parts_ref[s, b].astype(jnp.float32)
        delta = lax.dot_general(
            total.astype(jnp.bfloat16),
            up_ref[owner_ref[first + b]],
            (((0,), (0,)), ((), ())),
            preferred_element_type=jnp.float32,
        )
        span = pl.ds(b * rows, rows)
        out_ref[span, :] = (base_ref[span, :] + delta).astype(jnp.bfloat16)


def finish(owner, parts, ups, base):
    shares, blocks, rank, rows = parts.shape
    wide = base.shape[1]
    step = blocks // 2
    return pl.pallas_call(
        final_kernel,
        out_shape=jax.ShapeDtypeStruct(base.shape, jnp.bfloat16),
        grid=(blocks // step,),
        in_specs=[
            SMEM_SPEC,
            pl.BlockSpec((shares, step, rank, rows), lambda i: (0, i, 0, 0)),
            pl.BlockSpec(ups.shape, lambda i: (0, 0, 0)),
            pl.BlockSpec((step * rows, wide), lambda i: (i, 0)),
        ],
        out_specs=pl.BlockSpec((step * rows, wide), lambda i: (i, 0)),
        compiler_params=VMEM_LIMIT,
    )(owner, parts, ups, base)


def local(
    tokens, value_projection_weight, adapter_down_factors, adapter_up_factors, block_adapter_table
):
    groups = lax.axis_size("dp")
    rows_dev, feat_dev = tokens.shape
    blocks = rows_dev // BLOCK
    adapter_per_device = adapter_down_factors.shape[0]
    ids = block_adapter_table[0]
    owner = ids // adapter_per_device
    hit = owner[None, :] == jnp.arange(groups, dtype=jnp.int32)[:, None]
    asked = jnp.sum(jnp.where(hit, (ids - owner * adapter_per_device)[None, :], 0), axis=1)
    wanted = lax.all_to_all(asked[:, None], "dp", split_axis=0, concat_axis=0, tiled=True)
    outgoing = pick(wanted, jnp.swapaxes(adapter_down_factors, 1, 2))
    base_part = jnp.dot(tokens, value_projection_weight, preferred_element_type=jnp.float32)
    outgoing, base_part = lax.optimization_barrier((outgoing, base_part))
    received = lax.all_to_all(outgoing, "dp", split_axis=0, concat_axis=0, tiled=True)
    base = lax.psum_scatter(base_part, "tensor", scatter_dimension=1, tiled=True)
    outgoing_up = pick(wanted, adapter_up_factors)
    received, base, outgoing_up = lax.optimization_barrier((received, base, outgoing_up))
    ups = lax.all_to_all(outgoing_up, "dp", split_axis=0, concat_axis=0, tiled=True)
    part = down_products(owner, tokens.reshape(blocks, BLOCK, feat_dev), received)
    parts = lax.all_gather(part, "tensor", axis=0)
    return finish(owner, parts, ups, base)


def solution(mesh):
    placed = (
        P("dp", "tensor"),
        P("tensor", None),
        P("dp", "tensor", None),
        P("dp", None, "tensor"),
        P("dp", None),
    )
    return jax.shard_map(
        local, mesh=mesh, in_specs=placed, out_specs=P("dp", "tensor"), check_vma=False
    )
```

```python
import jax
import jax.numpy as jnp
from jax import lax
from jax.experimental import pallas as pl
from jax.experimental.pallas import tpu as pltpu
from jax.sharding import PartitionSpec as P

BLOCK = 128


VMEM_LIMIT = pltpu.CompilerParams(vmem_limit_bytes=62 * 1024 * 1024)
SMEM_SPEC = pl.BlockSpec(memory_space=pltpu.SMEM)
HBM_SPEC = pl.BlockSpec(memory_space=pltpu.HBM)
VMEM_SPEC = pl.BlockSpec(memory_space=pltpu.VMEM)


def pick_kernel(ids_ref, src_ref, out_ref, buf, insem, outsem):
    slots = buf.shape[0]
    groups = insem.shape[0]
    size = slots // groups
    for s in range(slots):
        pltpu.make_async_copy(src_ref.at[ids_ref[s, 0]], buf.at[s], insem.at[s // size]).start()
    stores = []
    for g in range(groups):
        span = pl.ds(g * size, size)
        pltpu.make_async_copy(src_ref.at[span], buf.at[span], insem.at[g]).wait()
        stores.append(pltpu.make_async_copy(buf.at[span], out_ref.at[span], outsem.at[g]))
        stores[g].start()
    for store in stores:
        store.wait()


def pick(ids, src):
    groups = 4
    shape = (ids.shape[0],) + src.shape[1:]
    return pl.pallas_call(
        pick_kernel,
        out_shape=jax.ShapeDtypeStruct(shape, src.dtype),
        in_specs=[SMEM_SPEC, HBM_SPEC],
        out_specs=HBM_SPEC,
        scratch_shapes=[
            pltpu.VMEM(shape, src.dtype),
            pltpu.SemaphoreType.DMA((groups,)),
            pltpu.SemaphoreType.DMA((groups,)),
        ],
        compiler_params=VMEM_LIMIT,
    )(ids, src)


def base_kernel(place_ref, tok_ref, wgt_ref, *rest):
    outs, cols = rest[:-1], rest[-1]
    steps = len(outs) // 2
    wide = outs[0].shape[1]
    y, core = place_ref[0], place_ref[1]

    @pl.when(pl.program_id(0) == 0)
    def _():
        for j in range(2 * steps):
            block = 2 * lax.rem(y + j % steps, steps) + (core if j < steps else 1 - core)
            start = pl.multiple_of(block * wide, wide)
            cols[:, j * wide : (j + 1) * wide] = wgt_ref[:, pl.ds(start, wide)]

    out = jnp.dot(tok_ref[...], cols[...], preferred_element_type=jnp.float32)
    for j in range(2 * steps):
        outs[j][...] = out[:, j * wide : (j + 1) * wide]


def base_products(place, tokens, weight, wide):
    rows, feat = tokens.shape
    values = weight.shape[1]
    tile = 256
    count = values // wide
    return pl.pallas_call(
        base_kernel,
        out_shape=tuple(jax.ShapeDtypeStruct((rows, wide), jnp.float32) for _ in range(count)),
        grid=(rows // tile,),
        in_specs=[
            SMEM_SPEC,
            pl.BlockSpec((tile, feat), lambda i: (i, 0)),
            pl.BlockSpec((feat, values), lambda i: (0, 0)),
        ],
        out_specs=tuple(pl.BlockSpec((tile, wide), lambda i: (i, 0)) for _ in range(count)),
        scratch_shapes=[pltpu.VMEM((feat, values), weight.dtype)],
        compiler_params=VMEM_LIMIT,
    )(place, tokens, weight)


def down_kernel(place_ref, owner_ref, tok_ref, recv_ref, keep_ref, give_ref, tok, fac, tsem, fsem):
    blocks = tok.shape[0]
    groups = tsem.shape[0]
    size = blocks // groups
    half = blocks // 2
    core = place_ref[1]
    firsts = []
    for g in range(groups):
        side = 1 - core if g * size < half else core
        firsts.append(side * half + g * size % half)
        first = pl.multiple_of(firsts[g], size)
        span = pl.ds(g * size, size)
        pltpu.make_async_copy(tok_ref.at[pl.ds(first, size)], tok.at[span], tsem.at[g]).start()
        for b in range(size):
            pltpu.make_async_copy(
                recv_ref.at[owner_ref[first + b]], fac.at[g * size + b], fsem.at[g]
            ).start()
    for g in range(groups):
        span = pl.ds(g * size, size)
        pltpu.make_async_copy(recv_ref.at[span], fac.at[span], fsem.at[g]).wait()
        pltpu.make_async_copy(tok_ref.at[span], tok.at[span], tsem.at[g]).wait()
        for b in range(g * size, (g + 1) * size):
            out = lax.dot_general(
                fac[b],
                tok[b],
                (((1,), (1,)), ((), ())),
                preferred_element_type=jnp.float32,
            )
            if b < half:
                give_ref[b] = out
            else:
                keep_ref[b - half] = out


def down_products(place, owner, token_blocks, recv):
    groups = 4
    blocks, rows, feat = token_blocks.shape
    rank = recv.shape[1]
    half = jax.ShapeDtypeStruct((blocks // 2, rank, rows), jnp.float32)
    return pl.pallas_call(
        down_kernel,
        out_shape=(half, half),
        in_specs=[SMEM_SPEC, SMEM_SPEC, HBM_SPEC, HBM_SPEC],
        out_specs=(VMEM_SPEC, VMEM_SPEC),
        scratch_shapes=[
            pltpu.VMEM((blocks, rows, feat), jnp.bfloat16),
            pltpu.VMEM((blocks, rank, feat), jnp.bfloat16),
            pltpu.SemaphoreType.DMA((groups,)),
            pltpu.SemaphoreType.DMA((groups,)),
        ],
        compiler_params=VMEM_LIMIT,
    )(place, owner, token_blocks, recv)


def final_kernel(place_ref, owner_ref, mine_ref, other_ref, up_ref, base_ref, out_ref):
    blocks, rank, rows = mine_ref.shape
    step = pl.program_id(0)
    own = step == place_ref[1]
    for b in range(blocks):
        low = jnp.where(own, mine_ref[b], other_ref[b])
        delta = lax.dot_general(
            low,
            up_ref[owner_ref[step * blocks + b]],
            (((0,), (0,)), ((), ())),
            preferred_element_type=jnp.float32,
        )
        span = pl.ds(b * rows, rows)
        out_ref[span, :] = (base_ref[span, :] + delta).astype(jnp.bfloat16)


def finish(place, owner, mine, other, ups, base):
    blocks, rank, rows = mine.shape
    wide = base.shape[1]
    half = pl.BlockSpec((blocks, rank, rows), lambda i: (0, 0, 0))
    return pl.pallas_call(
        final_kernel,
        out_shape=jax.ShapeDtypeStruct(base.shape, jnp.bfloat16),
        grid=(2,),
        in_specs=[
            SMEM_SPEC,
            SMEM_SPEC,
            half,
            half,
            pl.BlockSpec(ups.shape, lambda i: (0, 0, 0)),
            pl.BlockSpec((blocks * rows, wide), lambda i: (i, 0)),
        ],
        out_specs=pl.BlockSpec((blocks * rows, wide), lambda i: (i, 0)),
        compiler_params=VMEM_LIMIT,
    )(place, owner, mine, other, ups, base)


def local(
    tokens, value_projection_weight, adapter_down_factors, adapter_up_factors, block_adapter_table
):
    groups = lax.axis_size("dp")
    shares = lax.axis_size("tensor")
    chips = shares // 2
    me = lax.axis_index("tensor")
    place = jnp.stack([me // 2, me % 2]).astype(jnp.int32)
    swap = [(i, i ^ 1) for i in range(shares)]
    columns = [[2 * y + c for y in range(chips)] for c in range(2)]
    rows_dev, feat_dev = tokens.shape
    wide = adapter_up_factors.shape[2]
    blocks = rows_dev // BLOCK
    adapter_per_device = adapter_down_factors.shape[0]
    ids = block_adapter_table[0]
    owner = ids // adapter_per_device
    hit = owner[None, :] == jnp.arange(groups, dtype=jnp.int32)[:, None]
    asked = jnp.sum(jnp.where(hit, (ids - owner * adapter_per_device)[None, :], 0), axis=1)
    wanted = lax.all_to_all(asked[:, None], "dp", split_axis=0, concat_axis=0, tiled=True)
    outgoing = pick(wanted, jnp.swapaxes(adapter_down_factors, 1, 2))
    products = base_products(place, tokens, value_projection_weight, wide)
    outgoing, products = lax.optimization_barrier((outgoing, products))
    received = lax.all_to_all(outgoing, "dp", split_axis=0, concat_axis=0, tiled=True)

    sums = {}
    for k in (2, 1, 3, 0):
        sums[k] = products[k] + lax.ppermute(products[chips + k], "tensor", swap)
        if k:
            along = [(i, 2 * ((i // 2 + k) % chips) + i % 2) for i in range(shares)]
            sums[k] = lax.ppermute(sums[k], "tensor", along)
    base = (sums[0] + sums[1]) + (sums[2] + sums[3])

    outgoing_up = pick(wanted, adapter_up_factors)
    received, base, outgoing_up = lax.optimization_barrier((received, base, outgoing_up))
    ups = lax.all_to_all(outgoing_up, "dp", split_axis=0, concat_axis=0, tiled=True)
    keep, give = down_products(place, owner, tokens.reshape(blocks, BLOCK, feat_dev), received)
    part = (keep + lax.ppermute(give, "tensor", swap)).astype(jnp.bfloat16)
    parts = lax.all_gather(part, "tensor", axis=0, axis_index_groups=columns)
    mine = jnp.sum(parts.astype(jnp.float32), axis=0).astype(jnp.bfloat16)
    other = lax.ppermute(mine, "tensor", swap)
    return finish(place, owner, mine, other, ups, base)


def solution(mesh):
    placed = (
        P("dp", "tensor"),
        P("tensor", None),
        P("dp", "tensor", None),
        P("dp", None, "tensor"),
        P("dp", None),
    )
    return jax.shard_map(
        local, mesh=mesh, in_specs=placed, out_specs=P("dp", "tensor"), check_vma=False
    )
```

```python
import jax
import jax.numpy as jnp
from jax import lax
from jax.experimental import pallas as pl
from jax.experimental.pallas import tpu as pltpu
from jax.sharding import PartitionSpec as P

BLOCK = 128


def grant(mib):
    return pltpu.CompilerParams(vmem_limit_bytes=mib * 1024 * 1024)


SMEM_SPEC = pl.BlockSpec(memory_space=pltpu.SMEM)
HBM_SPEC = pl.BlockSpec(memory_space=pltpu.HBM)
VMEM_SPEC = pl.BlockSpec(memory_space=pltpu.VMEM)


def pick_kernel(ids_ref, src_ref, out_ref, sem):
    slots = out_ref.shape[0]
    for s in range(slots):
        pltpu.make_async_copy(src_ref.at[ids_ref[s, 0]], out_ref.at[s], sem).start()
    pltpu.make_async_copy(src_ref, out_ref, sem).wait()


def pick(ids, src):
    assert ids.shape[0] == src.shape[0]
    return pl.pallas_call(
        pick_kernel,
        out_shape=jax.ShapeDtypeStruct(src.shape, src.dtype),
        in_specs=[SMEM_SPEC, VMEM_SPEC],
        out_specs=HBM_SPEC,
        scratch_shapes=[pltpu.SemaphoreType.DMA(())],
        compiler_params=grant(52),
    )(ids, src)


def base_kernel(place_ref, tok_ref, wgt_ref, *rest):
    outs, cols = rest[:-1], rest[-1]
    steps = len(outs) // 2
    wide = outs[0].shape[1]
    y, core = place_ref[0], place_ref[1]

    @pl.when(pl.program_id(0) == 0)
    def _():
        for j in range(2 * steps):
            block = 2 * lax.rem(y + j % steps, steps) + (core if j < steps else 1 - core)
            start = pl.multiple_of(block * wide, wide)
            cols[:, j * wide : (j + 1) * wide] = wgt_ref[:, pl.ds(start, wide)]

    out = jnp.dot(tok_ref[...], cols[...], preferred_element_type=jnp.float32)
    for j in range(2 * steps):
        outs[j][...] = out[:, j * wide : (j + 1) * wide]


def base_products(place, tokens, weight, wide):
    rows, feat = tokens.shape
    values = weight.shape[1]
    tile = 256
    count = values // wide
    return pl.pallas_call(
        base_kernel,
        out_shape=tuple(jax.ShapeDtypeStruct((rows, wide), jnp.float32) for _ in range(count)),
        grid=(rows // tile,),
        in_specs=[
            SMEM_SPEC,
            pl.BlockSpec((tile, feat), lambda i: (i, 0)),
            pl.BlockSpec((feat, values), lambda i: (0, 0)),
        ],
        out_specs=tuple(pl.BlockSpec((tile, wide), lambda i: (i, 0)) for _ in range(count)),
        scratch_shapes=[pltpu.VMEM((feat, values), weight.dtype)],
        compiler_params=grant(20),
    )(place, tokens, weight)


def down_kernel(place_ref, owner_ref, tok_ref, recv_ref, keep_ref, give_ref, fac, sem):
    blocks = fac.shape[0]
    groups = sem.shape[0]
    size = blocks // groups
    half = blocks // 2
    core = place_ref[1]
    order = [(1 - core if b < half else core) * half + b % half for b in range(blocks)]
    for b in range(blocks):
        pltpu.make_async_copy(recv_ref.at[owner_ref[order[b]]], fac.at[b], sem.at[b // size]).start()
    for g in range(groups):
        span = pl.ds(g * size, size)
        pltpu.make_async_copy(recv_ref.at[span], fac.at[span], sem.at[g]).wait()
        for b in range(g * size, (g + 1) * size):
            out = lax.dot_general(
                fac[b],
                tok_ref[order[b]],
                (((1,), (1,)), ((), ())),
                preferred_element_type=jnp.float32,
            )
            if b < half:
                give_ref[b] = out
            else:
                keep_ref[b - half] = out


def down_products(place, owner, token_blocks, recv):
    groups = 4
    blocks, rows, feat = token_blocks.shape
    rank = recv.shape[1]
    half = jax.ShapeDtypeStruct((blocks // 2, rank, rows), jnp.float32)
    return pl.pallas_call(
        down_kernel,
        out_shape=(half, half),
        in_specs=[SMEM_SPEC, SMEM_SPEC, VMEM_SPEC, HBM_SPEC],
        out_specs=(VMEM_SPEC, VMEM_SPEC),
        scratch_shapes=[
            pltpu.VMEM((blocks, rank, feat), jnp.bfloat16),
            pltpu.SemaphoreType.DMA((groups,)),
        ],
        compiler_params=grant(52),
    )(place, owner, token_blocks, recv)


def final_kernel(place_ref, owner_ref, mine_ref, other_ref, up_ref, base_ref, out_ref):
    blocks, rank, rows = mine_ref.shape
    step = pl.program_id(0)
    own = step == place_ref[1]
    for b in range(blocks):
        low = jnp.where(own, mine_ref[b], other_ref[b])
        delta = lax.dot_general(
            low,
            up_ref[owner_ref[step * blocks + b]],
            (((0,), (0,)), ((), ())),
            preferred_element_type=jnp.float32,
        )
        span = pl.ds(b * rows, rows)
        out_ref[span, :] = (base_ref[span, :] + delta).astype(jnp.bfloat16)


def finish(place, owner, mine, other, ups, base):
    blocks, rank, rows = mine.shape
    wide = base.shape[1]
    half = pl.BlockSpec((blocks, rank, rows), lambda i: (0, 0, 0))
    return pl.pallas_call(
        final_kernel,
        out_shape=jax.ShapeDtypeStruct(base.shape, jnp.bfloat16),
        grid=(2,),
        in_specs=[
            SMEM_SPEC,
            SMEM_SPEC,
            half,
            half,
            pl.BlockSpec(ups.shape, lambda i: (0, 0, 0)),
            pl.BlockSpec((blocks * rows, wide), lambda i: (i, 0)),
        ],
        out_specs=pl.BlockSpec((blocks * rows, wide), lambda i: (i, 0)),
        compiler_params=grant(24),
    )(place, owner, mine, other, ups, base)


def local(
    tokens, value_projection_weight, adapter_down_factors, adapter_up_factors, block_adapter_table
):
    groups = lax.axis_size("dp")
    shares = lax.axis_size("tensor")
    chips = shares // 2
    me = lax.axis_index("tensor")
    place = jnp.stack([me // 2, me % 2]).astype(jnp.int32)
    swap = [(i, i ^ 1) for i in range(shares)]
    columns = [[2 * y + c for y in range(chips)] for c in range(2)]
    rows_dev, feat_dev = tokens.shape
    wide = adapter_up_factors.shape[2]
    blocks = rows_dev // BLOCK
    adapter_per_device = adapter_down_factors.shape[0]
    ids = block_adapter_table[0]
    owner = ids // adapter_per_device
    hit = owner[None, :] == jnp.arange(groups, dtype=jnp.int32)[:, None]
    asked = jnp.sum(jnp.where(hit, (ids - owner * adapter_per_device)[None, :], 0), axis=1)
    wanted = lax.all_to_all(asked[:, None], "dp", split_axis=0, concat_axis=0, tiled=True)
    outgoing = pick(wanted, jnp.swapaxes(adapter_down_factors, 1, 2))
    received = lax.all_to_all(outgoing, "dp", split_axis=0, concat_axis=0, tiled=True)

    tokens, outgoing_up = lax.optimization_barrier((tokens, pick(wanted, adapter_up_factors)))
    products = base_products(place, tokens, value_projection_weight, wide)
    sums = {}
    for k in (2, 1, 3, 0):
        sums[k] = products[k] + lax.ppermute(products[chips + k], "tensor", swap)
        if k:
            along = [(i, 2 * ((i // 2 + k) % chips) + i % 2) for i in range(shares)]
            sums[k] = lax.ppermute(sums[k], "tensor", along)
    base = (sums[0] + sums[1]) + (sums[2] + sums[3])

    received, base, outgoing_up = lax.optimization_barrier((received, base, outgoing_up))
    ups = lax.all_to_all(outgoing_up, "dp", split_axis=0, concat_axis=0, tiled=True)
    keep, give = down_products(place, owner, tokens.reshape(blocks, BLOCK, feat_dev), received)
    part = (keep + lax.ppermute(give, "tensor", swap)).astype(jnp.bfloat16)
    parts = lax.all_gather(part, "tensor", axis=0, axis_index_groups=columns)
    mine = jnp.sum(parts.astype(jnp.float32), axis=0).astype(jnp.bfloat16)
    other = lax.ppermute(mine, "tensor", swap)
    return finish(place, owner, mine, other, ups, base)


def solution(mesh):
    placed = (
        P("dp", "tensor"),
        P("tensor", None),
        P("dp", "tensor", None),
        P("dp", None, "tensor"),
        P("dp", None),
    )
    return jax.shard_map(
        local, mesh=mesh, in_specs=placed, out_specs=P("dp", "tensor"), check_vma=False
    )
```

```python
import jax
import jax.numpy as jnp
from jax import lax
from jax.experimental import pallas as pl
from jax.experimental.pallas import tpu as pltpu
from jax.sharding import PartitionSpec as P

BLOCK = 128


def grant(mib):
    return pltpu.CompilerParams(vmem_limit_bytes=mib * 1024 * 1024)


SMEM_SPEC = pl.BlockSpec(memory_space=pltpu.SMEM)
HBM_SPEC = pl.BlockSpec(memory_space=pltpu.HBM)
VMEM_SPEC = pl.BlockSpec(memory_space=pltpu.VMEM)


def pick_kernel(ids_ref, src_ref, out_ref, sem):
    slots = out_ref.shape[0]
    for s in range(slots):
        pltpu.make_async_copy(src_ref.at[ids_ref[s, 0]], out_ref.at[s], sem).start()
    pltpu.make_async_copy(src_ref, out_ref, sem).wait()


def pick(ids, src):
    assert ids.shape[0] == src.shape[0]
    return pl.pallas_call(
        pick_kernel,
        out_shape=jax.ShapeDtypeStruct(src.shape, src.dtype),
        in_specs=[SMEM_SPEC, VMEM_SPEC],
        out_specs=HBM_SPEC,
        scratch_shapes=[pltpu.SemaphoreType.DMA(())],
        compiler_params=grant(52),
    )(ids, src)


def base_kernel(place_ref, tok_ref, wgt_ref, *rest):
    outs, cols = rest[:-1], rest[-1]
    steps = len(outs) // 2
    wide = outs[0].shape[1]
    y, core = place_ref[0], place_ref[1]

    @pl.when(pl.program_id(0) == 0)
    def _():
        for j in range(2 * steps):
            block = 2 * lax.rem(y + j % steps, steps) + (core if j < steps else 1 - core)
            start = pl.multiple_of(block * wide, wide)
            cols[:, j * wide : (j + 1) * wide] = wgt_ref[:, pl.ds(start, wide)]

    out = jnp.dot(tok_ref[...], cols[...], preferred_element_type=jnp.float32)
    for j in range(2 * steps):
        outs[j][...] = out[:, j * wide : (j + 1) * wide]


def base_products(place, tokens, weight, wide):
    rows, feat = tokens.shape
    values = weight.shape[1]
    tile = 256
    count = values // wide
    return pl.pallas_call(
        base_kernel,
        out_shape=tuple(jax.ShapeDtypeStruct((rows, wide), jnp.float32) for _ in range(count)),
        grid=(rows // tile,),
        in_specs=[
            SMEM_SPEC,
            pl.BlockSpec((tile, feat), lambda i: (i, 0)),
            pl.BlockSpec((feat, values), lambda i: (0, 0)),
        ],
        out_specs=tuple(pl.BlockSpec((tile, wide), lambda i: (i, 0)) for _ in range(count)),
        scratch_shapes=[pltpu.VMEM((feat, values), weight.dtype)],
        compiler_params=grant(20),
    )(place, tokens, weight)


def down_kernel(place_ref, owner_ref, tok_ref, recv_ref, keep_ref, give_ref, fac, sem):
    blocks = fac.shape[0]
    groups = sem.shape[0]
    size = blocks // groups
    half = blocks // 2
    core = place_ref[1]
    order = [(1 - core if b < half else core) * half + b % half for b in range(blocks)]
    for b in range(blocks):
        pltpu.make_async_copy(recv_ref.at[owner_ref[order[b]]], fac.at[b], sem.at[b // size]).start()
    for g in range(groups):
        span = pl.ds(g * size, size)
        pltpu.make_async_copy(recv_ref.at[span], fac.at[span], sem.at[g]).wait()
        for b in range(g * size, (g + 1) * size):
            out = lax.dot_general(
                fac[b],
                tok_ref[order[b]],
                (((1,), (1,)), ((), ())),
                preferred_element_type=jnp.float32,
            )
            if b < half:
                give_ref[b] = out
            else:
                keep_ref[b - half] = out


def down_products(place, owner, token_blocks, recv):
    groups = 4
    blocks, rows, feat = token_blocks.shape
    rank = recv.shape[1]
    half = jax.ShapeDtypeStruct((blocks // 2, rank, rows), jnp.float32)
    return pl.pallas_call(
        down_kernel,
        out_shape=(half, half),
        in_specs=[SMEM_SPEC, SMEM_SPEC, VMEM_SPEC, HBM_SPEC],
        out_specs=(VMEM_SPEC, VMEM_SPEC),
        scratch_shapes=[
            pltpu.VMEM((blocks, rank, feat), jnp.bfloat16),
            pltpu.SemaphoreType.DMA((groups,)),
        ],
        compiler_params=grant(52),
    )(place, owner, token_blocks, recv)


def final_kernel(place_ref, owner_ref, mine_ref, other_ref, up_ref, base_ref, out_ref):
    blocks, rank, rows = mine_ref.shape
    step = pl.program_id(0)
    own = step == place_ref[1]
    for b in range(blocks):
        low = jnp.where(own, mine_ref[b], other_ref[b])
        delta = lax.dot_general(
            low,
            up_ref[owner_ref[step * blocks + b]],
            (((0,), (0,)), ((), ())),
            preferred_element_type=jnp.float32,
        )
        span = pl.ds(b * rows, rows)
        out_ref[span, :] = (base_ref[span, :] + delta).astype(jnp.bfloat16)


def finish(place, owner, mine, other, ups, base):
    blocks, rank, rows = mine.shape
    wide = base.shape[1]
    half = pl.BlockSpec((blocks, rank, rows), lambda i: (0, 0, 0))
    return pl.pallas_call(
        final_kernel,
        out_shape=jax.ShapeDtypeStruct(base.shape, jnp.bfloat16),
        grid=(2,),
        in_specs=[
            SMEM_SPEC,
            SMEM_SPEC,
            half,
            half,
            pl.BlockSpec(ups.shape, lambda i: (0, 0, 0)),
            pl.BlockSpec((blocks * rows, wide), lambda i: (i, 0)),
        ],
        out_specs=pl.BlockSpec((blocks * rows, wide), lambda i: (i, 0)),
        compiler_params=grant(24),
    )(place, owner, mine, other, ups, base)


def local(
    tokens, value_projection_weight, adapter_down_factors, adapter_up_factors, block_adapter_table
):
    groups = lax.axis_size("dp")
    shares = lax.axis_size("tensor")
    chips = shares // 2
    me = lax.axis_index("tensor")
    place = jnp.stack([me // 2, me % 2]).astype(jnp.int32)
    swap = [(i, i ^ 1) for i in range(shares)]
    columns = [[2 * y + c for y in range(chips)] for c in range(2)]
    rows_dev, feat_dev = tokens.shape
    wide = adapter_up_factors.shape[2]
    blocks = rows_dev // BLOCK
    adapter_per_device = adapter_down_factors.shape[0]
    ids = block_adapter_table[0]
    owner = ids // adapter_per_device
    hit = owner[None, :] == jnp.arange(groups, dtype=jnp.int32)[:, None]
    asked = jnp.sum(jnp.where(hit, (ids - owner * adapter_per_device)[None, :], 0), axis=1)
    wanted = lax.all_to_all(asked[:, None], "dp", split_axis=0, concat_axis=0, tiled=True)
    lines = 4
    layers = groups // lines
    my_line = lax.axis_index("dp") % lines
    ring = jnp.arange(lines, dtype=jnp.int32)
    outgoing = pick(wanted, jnp.swapaxes(adapter_down_factors, 1, 2))
    received = lax.all_to_all(outgoing, "dp", split_axis=0, concat_axis=0, tiled=True)

    by_line = wanted.reshape(layers, lines)[:, (my_line + ring) % lines].T.reshape(groups, 1)
    up_lines = pick(by_line, adapter_up_factors).reshape((lines, layers) + adapter_up_factors.shape[1:])
    tokens, up_lines = lax.optimization_barrier((tokens, up_lines))
    moved = [up_lines[0]]
    for d in range(1, lines):
        along = [(i, i - i % lines + (i + d) % lines) for i in range(groups)]
        moved.append(lax.ppermute(up_lines[d], "dp", along))
    outgoing_up = jnp.stack(moved, axis=1)
    products = base_products(place, tokens, value_projection_weight, wide)
    sums = {}
    for k in (2, 1, 3, 0):
        sums[k] = products[k] + lax.ppermute(products[chips + k], "tensor", swap)
        if k:
            along = [(i, 2 * ((i // 2 + k) % chips) + i % 2) for i in range(shares)]
            sums[k] = lax.ppermute(sums[k], "tensor", along)
    base = (sums[0] + sums[1]) + (sums[2] + sums[3])

    received, base, outgoing_up = lax.optimization_barrier((received, base, outgoing_up))
    columns_z = [[z * lines + x for z in range(layers)] for x in range(lines)]
    ups = lax.all_to_all(
        outgoing_up, "dp", split_axis=0, concat_axis=0, tiled=True, axis_index_groups=columns_z
    ).reshape((groups,) + adapter_up_factors.shape[1:])
    up_slot = owner - owner % lines + (my_line - owner % lines) % lines
    keep, give = down_products(place, owner, tokens.reshape(blocks, BLOCK, feat_dev), received)
    part = (keep + lax.ppermute(give, "tensor", swap)).astype(jnp.bfloat16)
    parts = lax.all_gather(part, "tensor", axis=0, axis_index_groups=columns)
    mine = jnp.sum(parts.astype(jnp.float32), axis=0).astype(jnp.bfloat16)
    other = lax.ppermute(mine, "tensor", swap)
    return finish(place, up_slot, mine, other, ups, base)


def solution(mesh):
    placed = (
        P("dp", "tensor"),
        P("tensor", None),
        P("dp", "tensor", None),
        P("dp", None, "tensor"),
        P("dp", None),
    )
    return jax.shard_map(
        local, mesh=mesh, in_specs=placed, out_specs=P("dp", "tensor"), check_vma=False
    )
```

```python
import jax
import jax.numpy as jnp
from jax import lax
from jax.experimental import pallas as pl
from jax.experimental.pallas import tpu as pltpu
from jax.sharding import PartitionSpec as P

BLOCK = 128


def grant(mib):
    return pltpu.CompilerParams(vmem_limit_bytes=mib * 1024 * 1024)


SMEM_SPEC = pl.BlockSpec(memory_space=pltpu.SMEM)
HBM_SPEC = pl.BlockSpec(memory_space=pltpu.HBM)
VMEM_SPEC = pl.BlockSpec(memory_space=pltpu.VMEM)


def ask_kernel(table_ref, out_ref):
    groups, _, lanes = out_ref.shape
    share = out_ref.shape[0]
    table = table_ref[...]
    blocks = table.shape[1]
    owner = lax.broadcasted_iota(jnp.int32, (groups, blocks), 0)
    inside = jnp.broadcast_to(table, (groups, blocks)) - owner * share
    hit = (inside >= 0) & (inside < share)
    asked = jnp.sum(jnp.where(hit, inside, 0), axis=1, keepdims=True)
    out_ref[...] = jnp.broadcast_to(asked, (groups, lanes)).reshape(groups, 1, lanes)


def ask(table, groups, share):
    assert groups == share
    return pl.pallas_call(
        ask_kernel,
        out_shape=jax.ShapeDtypeStruct((groups, 1, 128), jnp.int32),
        in_specs=[VMEM_SPEC],
        out_specs=VMEM_SPEC,
        compiler_params=grant(2),
    )(table)


def pick_kernel(ids_ref, src_ref, out_ref, sem):
    slots = out_ref.shape[0]
    for s in range(slots):
        pltpu.make_async_copy(src_ref.at[ids_ref[s, 0, 0]], out_ref.at[s], sem).start()
    pltpu.make_async_copy(src_ref, out_ref, sem).wait()


def pick(ids, src):
    assert ids.shape[0] == src.shape[0]
    return pl.pallas_call(
        pick_kernel,
        out_shape=jax.ShapeDtypeStruct(src.shape, src.dtype),
        in_specs=[SMEM_SPEC, VMEM_SPEC],
        out_specs=HBM_SPEC,
        scratch_shapes=[pltpu.SemaphoreType.DMA(())],
        compiler_params=grant(52),
    )(ids, src)


def base_kernel(place_ref, tok_ref, wgt_ref, *rest):
    outs, cols = rest[:-1], rest[-1]
    steps = len(outs) // 2
    wide = outs[0].shape[1]
    y, core = place_ref[0], place_ref[1]

    @pl.when(pl.program_id(0) == 0)
    def _():
        for j in range(2 * steps):
            block = 2 * lax.rem(y + j % steps, steps) + (core if j < steps else 1 - core)
            start = pl.multiple_of(block * wide, wide)
            cols[:, j * wide : (j + 1) * wide] = wgt_ref[:, pl.ds(start, wide)]

    out = jnp.dot(tok_ref[...], cols[...], preferred_element_type=jnp.float32)
    for j in range(2 * steps):
        outs[j][...] = out[:, j * wide : (j + 1) * wide]


def base_products(place, tokens, weight, wide):
    rows, feat = tokens.shape
    values = weight.shape[1]
    tile = 256
    count = values // wide
    return pl.pallas_call(
        base_kernel,
        out_shape=tuple(jax.ShapeDtypeStruct((rows, wide), jnp.float32) for _ in range(count)),
        grid=(rows // tile,),
        in_specs=[
            SMEM_SPEC,
            pl.BlockSpec((tile, feat), lambda i: (i, 0)),
            pl.BlockSpec((feat, values), lambda i: (0, 0)),
        ],
        out_specs=tuple(pl.BlockSpec((tile, wide), lambda i: (i, 0)) for _ in range(count)),
        scratch_shapes=[pltpu.VMEM((feat, values), weight.dtype)],
        compiler_params=grant(20),
    )(place, tokens, weight)


def down_kernel(place_ref, owner_ref, tok_ref, recv_ref, keep_ref, give_ref, fac, sem):
    blocks = fac.shape[0]
    groups = sem.shape[0]
    size = blocks // groups
    half = blocks // 2
    core = place_ref[1]
    order = [(1 - core if b < half else core) * half + b % half for b in range(blocks)]
    for b in range(blocks):
        pltpu.make_async_copy(recv_ref.at[owner_ref[order[b]]], fac.at[b], sem.at[b // size]).start()
    for g in range(groups):
        span = pl.ds(g * size, size)
        pltpu.make_async_copy(recv_ref.at[span], fac.at[span], sem.at[g]).wait()
        first = pl.multiple_of(order[g * size], size)
        rank, feat = fac.shape[1:]
        rows = tok_ref.shape[1]
        out = lax.dot_general(
            fac[span].reshape(size * rank, feat),
            tok_ref[pl.ds(first, size)].reshape(size * rows, feat),
            (((1,), (1,)), ((), ())),
            preferred_element_type=jnp.float32,
        )
        for j in range(size):
            b = g * size + j
            pair = out[j * rank : (j + 1) * rank, j * rows : (j + 1) * rows]
            if b < half:
                give_ref[b] = pair
            else:
                keep_ref[b - half] = pair


def down_products(place, owner, token_blocks, recv):
    groups = 4
    blocks, rows, feat = token_blocks.shape
    rank = recv.shape[1]
    half = jax.ShapeDtypeStruct((blocks // 2, rank, rows), jnp.float32)
    return pl.pallas_call(
        down_kernel,
        out_shape=(half, half),
        in_specs=[SMEM_SPEC, SMEM_SPEC, VMEM_SPEC, HBM_SPEC],
        out_specs=(VMEM_SPEC, VMEM_SPEC),
        scratch_shapes=[
            pltpu.VMEM((blocks, rank, feat), jnp.bfloat16),
            pltpu.SemaphoreType.DMA((groups,)),
        ],
        compiler_params=grant(52),
    )(place, owner, token_blocks, recv)


def final_kernel(place_ref, owner_ref, mine_ref, other_ref, up_ref, base_ref, out_ref):
    blocks, rank, rows = mine_ref.shape
    step = pl.program_id(0)
    own = step == place_ref[1]
    for b in range(blocks):
        low = jnp.where(own, mine_ref[b], other_ref[b])
        delta = lax.dot_general(
            low,
            up_ref[owner_ref[step * blocks + b]],
            (((0,), (0,)), ((), ())),
            preferred_element_type=jnp.float32,
        )
        span = pl.ds(b * rows, rows)
        out_ref[span, :] = (base_ref[span, :] + delta).astype(jnp.bfloat16)


def finish(place, owner, mine, other, ups, base):
    blocks, rank, rows = mine.shape
    wide = base.shape[1]
    half = pl.BlockSpec((blocks, rank, rows), lambda i: (0, 0, 0))
    return pl.pallas_call(
        final_kernel,
        out_shape=jax.ShapeDtypeStruct(base.shape, jnp.bfloat16),
        grid=(2,),
        in_specs=[
            SMEM_SPEC,
            SMEM_SPEC,
            half,
            half,
            pl.BlockSpec(ups.shape, lambda i: (0, 0, 0)),
            pl.BlockSpec((blocks * rows, wide), lambda i: (i, 0)),
        ],
        out_specs=pl.BlockSpec((blocks * rows, wide), lambda i: (i, 0)),
        compiler_params=grant(24),
    )(place, owner, mine, other, ups, base)


def local(
    tokens, value_projection_weight, adapter_down_factors, adapter_up_factors, block_adapter_table
):
    groups = lax.axis_size("dp")
    shares = lax.axis_size("tensor")
    chips = shares // 2
    me = lax.axis_index("tensor")
    place = jnp.stack([me // 2, me % 2]).astype(jnp.int32)
    swap = [(i, i ^ 1) for i in range(shares)]
    columns = [[2 * y + c for y in range(chips)] for c in range(2)]
    rows_dev, feat_dev = tokens.shape
    wide = adapter_up_factors.shape[2]
    blocks = rows_dev // BLOCK
    adapter_per_device = adapter_down_factors.shape[0]
    ids = block_adapter_table[0]
    owner = ids // adapter_per_device
    asked = ask(block_adapter_table, groups, adapter_per_device)
    wanted = lax.all_to_all(asked, "dp", split_axis=0, concat_axis=0, tiled=True)
    lines = 4
    layers = groups // lines
    my_line = lax.axis_index("dp") % lines
    ring = jnp.arange(lines, dtype=jnp.int32)
    outgoing = pick(wanted, jnp.swapaxes(adapter_down_factors, 1, 2))
    received = lax.all_to_all(outgoing, "dp", split_axis=0, concat_axis=0, tiled=True)

    by_line = wanted.reshape(layers, lines, -1)[:, (my_line + ring) % lines]
    by_line = jnp.swapaxes(by_line, 0, 1).reshape(wanted.shape)
    up_lines = pick(by_line, adapter_up_factors).reshape((lines, layers) + adapter_up_factors.shape[1:])
    tokens, up_lines = lax.optimization_barrier((tokens, up_lines))
    moved = [up_lines[0]]
    for d in range(1, lines):
        along = [(i, i - i % lines + (i + d) % lines) for i in range(groups)]
        moved.append(lax.ppermute(up_lines[d], "dp", along))
    outgoing_up = jnp.stack(moved, axis=1)
    products = base_products(place, tokens, value_projection_weight, wide)
    sums = {}
    for k in (2, 1, 3, 0):
        sums[k] = products[k] + lax.ppermute(products[chips + k], "tensor", swap)
        if k:
            along = [(i, 2 * ((i // 2 + k) % chips) + i % 2) for i in range(shares)]
            sums[k] = lax.ppermute(sums[k], "tensor", along)
    base = (sums[0] + sums[1]) + (sums[2] + sums[3])

    received, base, outgoing_up = lax.optimization_barrier((received, base, outgoing_up))
    columns_z = [[z * lines + x for z in range(layers)] for x in range(lines)]
    ups = lax.all_to_all(
        outgoing_up, "dp", split_axis=0, concat_axis=0, tiled=True, axis_index_groups=columns_z
    ).reshape((groups,) + adapter_up_factors.shape[1:])
    up_slot = owner - owner % lines + (my_line - owner % lines) % lines
    keep, give = down_products(place, owner, tokens.reshape(blocks, BLOCK, feat_dev), received)
    part = (keep + lax.ppermute(give, "tensor", swap)).astype(jnp.bfloat16)
    parts = lax.all_gather(part, "tensor", axis=0, axis_index_groups=columns)
    mine = jnp.sum(parts.astype(jnp.float32), axis=0).astype(jnp.bfloat16)
    other = lax.ppermute(mine, "tensor", swap)
    return finish(place, up_slot, mine, other, ups, base)


def solution(mesh):
    placed = (
        P("dp", "tensor"),
        P("tensor", None),
        P("dp", "tensor", None),
        P("dp", None, "tensor"),
        P("dp", None),
    )
    return jax.shard_map(
        local, mesh=mesh, in_specs=placed, out_specs=P("dp", "tensor"), check_vma=False
    )
```

```python
import jax
import jax.numpy as jnp
from jax import lax
from jax.experimental import pallas as pl
from jax.experimental.pallas import tpu as pltpu
from jax.sharding import PartitionSpec as P

BLOCK = 128


def grant(mib):
    return pltpu.CompilerParams(vmem_limit_bytes=mib * 1024 * 1024)


SMEM_SPEC = pl.BlockSpec(memory_space=pltpu.SMEM)
HBM_SPEC = pl.BlockSpec(memory_space=pltpu.HBM)
VMEM_SPEC = pl.BlockSpec(memory_space=pltpu.VMEM)


def pick_kernel(ids_ref, src_ref, out_ref, sem):
    slots = out_ref.shape[0]
    for s in range(slots):
        pltpu.make_async_copy(src_ref.at[ids_ref[s, 0]], out_ref.at[s], sem).start()
    pltpu.make_async_copy(src_ref, out_ref, sem).wait()


def pick(ids, src):
    assert ids.shape[0] == src.shape[0]
    return pl.pallas_call(
        pick_kernel,
        out_shape=jax.ShapeDtypeStruct(src.shape, src.dtype),
        in_specs=[SMEM_SPEC, VMEM_SPEC],
        out_specs=HBM_SPEC,
        scratch_shapes=[pltpu.SemaphoreType.DMA(())],
        compiler_params=grant(52),
    )(ids, src)


def base_kernel(place_ref, tok_ref, wgt_ref, *rest):
    outs, cols = rest[:-1], rest[-1]
    steps = len(outs) // 2
    wide = outs[0].shape[1]
    y, core = place_ref[0], place_ref[1]

    @pl.when(pl.program_id(0) == 0)
    def _():
        for j in range(2 * steps):
            block = 2 * lax.rem(y + j % steps, steps) + (core if j < steps else 1 - core)
            start = pl.multiple_of(block * wide, wide)
            cols[:, j * wide : (j + 1) * wide] = wgt_ref[:, pl.ds(start, wide)]

    out = jnp.dot(tok_ref[...], cols[...], preferred_element_type=jnp.float32)
    for j in range(2 * steps):
        outs[j][...] = out[:, j * wide : (j + 1) * wide]


def base_products(place, tokens, weight, wide):
    rows, feat = tokens.shape
    values = weight.shape[1]
    tile = 256
    count = values // wide
    return pl.pallas_call(
        base_kernel,
        out_shape=tuple(jax.ShapeDtypeStruct((rows, wide), jnp.float32) for _ in range(count)),
        grid=(rows // tile,),
        in_specs=[
            SMEM_SPEC,
            pl.BlockSpec((tile, feat), lambda i: (i, 0)),
            pl.BlockSpec((feat, values), lambda i: (0, 0)),
        ],
        out_specs=tuple(pl.BlockSpec((tile, wide), lambda i: (i, 0)) for _ in range(count)),
        scratch_shapes=[pltpu.VMEM((feat, values), weight.dtype)],
        compiler_params=grant(20),
    )(place, tokens, weight)


def down_kernel(place_ref, owner_ref, tok_ref, recv_ref, keep_ref, give_ref, fac, sem):
    blocks = fac.shape[0]
    groups = sem.shape[0]
    size = blocks // groups
    half = blocks // 2
    core = place_ref[1]
    order = [(1 - core if b < half else core) * half + b % half for b in range(blocks)]
    for b in range(blocks):
        pltpu.make_async_copy(recv_ref.at[owner_ref[order[b]]], fac.at[b], sem.at[b // size]).start()
    for g in range(groups):
        span = pl.ds(g * size, size)
        pltpu.make_async_copy(recv_ref.at[span], fac.at[span], sem.at[g]).wait()
        for b in range(g * size, (g + 1) * size):
            out = lax.dot_general(
                fac[b],
                tok_ref[order[b]],
                (((1,), (1,)), ((), ())),
                preferred_element_type=jnp.float32,
            )
            if b < half:
                give_ref[b] = out
            else:
                keep_ref[b - half] = out


def down_products(place, owner, token_blocks, recv):
    groups = 4
    blocks, rows, feat = token_blocks.shape
    rank = recv.shape[1]
    half = jax.ShapeDtypeStruct((blocks // 2, rank, rows), jnp.float32)
    return pl.pallas_call(
        down_kernel,
        out_shape=(half, half),
        in_specs=[SMEM_SPEC, SMEM_SPEC, VMEM_SPEC, HBM_SPEC],
        out_specs=(VMEM_SPEC, VMEM_SPEC),
        scratch_shapes=[
            pltpu.VMEM((blocks, rank, feat), jnp.bfloat16),
            pltpu.SemaphoreType.DMA((groups,)),
        ],
        compiler_params=grant(52),
    )(place, owner, token_blocks, recv)


def final_kernel(place_ref, owner_ref, mine_ref, other_ref, up_ref, base_ref, out_ref):
    blocks, rank, rows = mine_ref.shape
    step = pl.program_id(0)
    own = step == place_ref[1]
    for b in range(blocks):
        low = jnp.where(own, mine_ref[b], other_ref[b])
        delta = lax.dot_general(
            low,
            up_ref[owner_ref[step * blocks + b]],
            (((0,), (0,)), ((), ())),
            preferred_element_type=jnp.float32,
        )
        span = pl.ds(b * rows, rows)
        out_ref[span, :] = (base_ref[span, :] + delta).astype(jnp.bfloat16)


def finish(place, owner, mine, other, ups, base):
    blocks, rank, rows = mine.shape
    wide = base.shape[1]
    half = pl.BlockSpec((blocks, rank, rows), lambda i: (0, 0, 0))
    return pl.pallas_call(
        final_kernel,
        out_shape=jax.ShapeDtypeStruct(base.shape, jnp.bfloat16),
        grid=(2,),
        in_specs=[
            SMEM_SPEC,
            SMEM_SPEC,
            half,
            half,
            pl.BlockSpec(ups.shape, lambda i: (0, 0, 0)),
            pl.BlockSpec((blocks * rows, wide), lambda i: (i, 0)),
        ],
        out_specs=pl.BlockSpec((blocks * rows, wide), lambda i: (i, 0)),
        compiler_params=grant(24),
    )(place, owner, mine, other, ups, base)


def local(
    tokens, value_projection_weight, adapter_down_factors, adapter_up_factors, block_adapter_table
):
    groups = lax.axis_size("dp")
    shares = lax.axis_size("tensor")
    chips = shares // 2
    me = lax.axis_index("tensor")
    place = jnp.stack([me // 2, me % 2]).astype(jnp.int32)
    swap = [(i, i ^ 1) for i in range(shares)]
    columns = [[2 * y + c for y in range(chips)] for c in range(2)]
    rows_dev, feat_dev = tokens.shape
    wide = adapter_up_factors.shape[2]
    blocks = rows_dev // BLOCK
    adapter_per_device = adapter_down_factors.shape[0]
    ids = block_adapter_table[0]
    owner = ids // adapter_per_device
    hit = owner[None, :] == jnp.arange(groups, dtype=jnp.int32)[:, None]
    asked = jnp.sum(jnp.where(hit, (ids - owner * adapter_per_device)[None, :], 0), axis=1)
    wanted = lax.all_to_all(asked[:, None], "dp", split_axis=0, concat_axis=0, tiled=True)
    lines = 4
    layers = groups // lines
    my_line = lax.axis_index("dp") % lines
    ring = jnp.arange(lines, dtype=jnp.int32)
    outgoing = pick(wanted, jnp.swapaxes(adapter_down_factors, 1, 2))
    received = lax.all_to_all(outgoing, "dp", split_axis=0, concat_axis=0, tiled=True)

    by_line = wanted.reshape(layers, lines)[:, (my_line + ring) % lines].T.reshape(groups, 1)
    up_lines = pick(by_line, adapter_up_factors).reshape((lines, layers) + adapter_up_factors.shape[1:])
    tokens, up_lines = lax.optimization_barrier((tokens, up_lines))
    moved = [up_lines[0]]
    for d in range(1, lines):
        along = [(i, i - i % lines + (i + d) % lines) for i in range(groups)]
        moved.append(lax.ppermute(up_lines[d], "dp", along))
    outgoing_up = jnp.stack(moved, axis=1)
    products = base_products(place, tokens, value_projection_weight, wide)
    sums = {}
    for k in (2, 1, 3, 0):
        sums[k] = products[k] + lax.ppermute(products[chips + k], "tensor", swap)
        if k:
            along = [(i, 2 * ((i // 2 + k) % chips) + i % 2) for i in range(shares)]
            sums[k] = lax.ppermute(sums[k], "tensor", along)
    base = (sums[0] + sums[1]) + (sums[2] + sums[3])

    received, base, outgoing_up = lax.optimization_barrier((received, base, outgoing_up))
    up_slot = owner - owner % lines + (my_line - owner % lines) % lines
    keep, give = down_products(place, owner, tokens.reshape(blocks, BLOCK, feat_dev), received)
    keep, give, outgoing_up = lax.optimization_barrier((keep, give, outgoing_up))
    columns_z = [[z * lines + x for z in range(layers)] for x in range(lines)]
    ups = lax.all_to_all(
        outgoing_up, "dp", split_axis=0, concat_axis=0, tiled=True, axis_index_groups=columns_z
    ).reshape((groups,) + adapter_up_factors.shape[1:])
    part = (keep + lax.ppermute(give, "tensor", swap)).astype(jnp.bfloat16)
    parts = lax.all_gather(part, "tensor", axis=0, axis_index_groups=columns)
    mine = jnp.sum(parts.astype(jnp.float32), axis=0).astype(jnp.bfloat16)
    other = lax.ppermute(mine, "tensor", swap)
    return finish(place, up_slot, mine, other, ups, base)


def solution(mesh):
    placed = (
        P("dp", "tensor"),
        P("tensor", None),
        P("dp", "tensor", None),
        P("dp", None, "tensor"),
        P("dp", None),
    )
    return jax.shard_map(
        local, mesh=mesh, in_specs=placed, out_specs=P("dp", "tensor"), check_vma=False
    )
```
